32 devices in a mesh: ctx: 8 (over z, x), tp: 2 (over y), pp: 2 (over core).
Axes of the slice: x: 2, y: 2, z: 4, core: 2. Of those that a mesh axis runs over, the one named last changes fastest.
Arguments:
- features: bfloat16 [2, 2048, 3, 8192], P('pp', 'ctx', None, 'tp'), may hold values from -6 to 6
- short_taps: float32 [2, 3, 3, 8192], P('pp', None, None, 'tp'), may hold values from -3 to 3
- long_filters: bfloat16 [2, 128, 512], P('pp', None, 'tp'), may hold values from -0.5 to 0.5
- out_weight: bfloat16 [2, 8192, 4096], P('pp', 'tp', 'ctx'), may hold values from -0.09375 to 0.09375
- out_grad: bfloat16 [2, 2048, 4096], P('pp', 'ctx', 'tp'), may hold values from -6 to 6
Outputs:
- received_adjoint: bfloat16 [2, 2048, 3, 8192], P('pp', 'ctx', None, 'tp')
The draws below stay inside these ranges and needn't reach their ends.
All inputs are finite; a program needn't handle non-finite values.
Results may differ from the reference program's by a relative error of at most 0.013.
Values may be sent and summed in bfloat16 or wider, within the bound.
A program may use at most 192 MiB of HBM per device.

```python
import jax
import jax.numpy as jnp
from jax import lax

D = 8192
GROUP_CH = 16
FILT = 128
DOUT = 4096
GROUPS = 512
TOKENS = 2048
SECTIONS = 2


def levels(stream_key, shape, cuts, smallest, high):
    gain, own = 1.0, jax.random.fold_in(stream_key, 6)
    for dim, blocks in cuts:
        heights = jnp.exp(jax.random.uniform(jax.random.fold_in(own, dim), (blocks,), jnp.float32, smallest / len(cuts), high / len(cuts)))
        gain = gain * jnp.repeat(heights, shape[dim] // blocks).reshape([-1 if axis == dim else 1 for axis in range(len(shape))])
    return gain


def scatter_about(key, extent, scale, most, cuts=(), held_as=jnp.bfloat16):
    entries = scale * jax.random.normal(key, extent, jnp.float32)
    if cuts:
        entries = entries * levels(key, extent, cuts, -0.22, 0.18)
    return jnp.clip(entries, -most, most).astype(held_as)


def setup_inputs(seed: int = 0) -> dict:
    key_list = jax.random.split(jax.random.key(seed), 6)
    features = scatter_about(key_list[0], (SECTIONS, TOKENS, 3, D), 1.0, 6.0, ((0, 2), (1, 8), (3, 2)))
    short_taps = scatter_about(key_list[1], (SECTIONS, 3, 3, D), 0.6, 3.0, ((0, 2), (3, 2)), jnp.float32)
    long_filters = scatter_about(key_list[2], (SECTIONS, FILT, GROUPS), 0.09, 0.5, ((0, 2), (2, 2)))
    out_weight = scatter_about(key_list[3], (SECTIONS, D, DOUT), DOUT ** -0.5, 0.09375, ((0, 2), (1, 2), (2, 8)))
    out_grad = scatter_about(key_list[4], (SECTIONS, TOKENS, DOUT), 1.0, 6.0, ((0, 2), (1, 8), (2, 2)))
    return dict(features=features, short_taps=short_taps, long_filters=long_filters, out_weight=out_weight, out_grad=out_grad)


def one_section(feats, short_taps, filters, weight, cotangent):
    count = feats.shape[0]
    feat_f = feats.astype(jnp.float32)
    padded = jnp.pad(feat_f, ((2, 0), (0, 0), (0, 0)))
    mixed = short_taps[0] * padded[2:] + short_taps[1] * padded[1:-1] + short_taps[2] * padded[:-2]
    gate_part = mixed[:, 0]
    key_part = mixed[:, 1]
    value_part = mixed[:, 2]
    products = (key_part * value_part).astype(jnp.bfloat16)
    filt_chan = jnp.repeat(filters.astype(jnp.float32), GROUP_CH, axis=1)
    prod_pad = jnp.pad(products.astype(jnp.float32), ((FILT - 1, 0), (0, 0)))

    def fwd_tap(j, acc):
        return acc + filt_chan[j] * lax.dynamic_slice_in_dim(prod_pad, FILT - 1 - j, count, 0)

    conv_out = lax.fori_loop(0, FILT, fwd_tap, jnp.zeros(gate_part.shape, jnp.float32))
    grad_y = jnp.dot(cotangent, weight.T, preferred_element_type=jnp.float32).astype(jnp.bfloat16)
    grad_yf = grad_y.astype(jnp.float32)
    grad_gate = grad_yf * conv_out
    grad_conv = (grad_yf * gate_part).astype(jnp.bfloat16)
    conv_pad = jnp.pad(grad_conv.astype(jnp.float32), ((0, FILT - 1), (0, 0)))

    def bwd_tap(j, acc):
        return acc + filt_chan[j] * lax.dynamic_slice_in_dim(conv_pad, j, count, 0)

    grad_prod = lax.fori_loop(0, FILT, bwd_tap, jnp.zeros(gate_part.shape, jnp.float32))
    grad_mix = jnp.stack([grad_gate, grad_prod * value_part, grad_prod * key_part], axis=1).astype(jnp.bfloat16)
    mix_pad = jnp.pad(grad_mix.astype(jnp.float32), ((0, 2), (0, 0), (0, 0)))
    grad_feat = short_taps[0] * mix_pad[:count] + short_taps[1] * mix_pad[1:count + 1] + short_taps[2] * mix_pad[2:]
    return grad_feat.astype(jnp.bfloat16)


def reference(features, short_taps, long_filters, out_weight, out_grad):
    results = []
    for section in range(SECTIONS):
        results.append(one_section(features[section], short_taps[section], long_filters[section], out_weight[section], out_grad[section]))
    return jnp.stack([results[(section + 1) % SECTIONS] for section in range(SECTIONS)])
```

```python
import functools

import jax
import jax.numpy as jnp
from jax import lax
from jax.experimental import pallas as pl
from jax.experimental.pallas import tpu as pltpu
from jax.sharding import PartitionSpec as P

LANES = 128
TAIL = 8
CHUNKS = 4
F32 = jnp.float32
BF16 = jnp.bfloat16


def split_of(count):
    inner = 1
    while inner * inner * 4 <= count:
        inner *= 2
    return count // inner, inner


def ahead(block, axis, distance):
    devices = range(lax.axis_size(axis))
    return lax.ppermute(block, axis, [(i - distance, i) for i in devices if i - distance in devices])


def toeplitz(row, rows, shift):
    wide = jnp.broadcast_to(row, (rows, row.shape[1]))
    return pltpu.roll(wide, shift, 1, stride=1, stride_axis=0).astype(BF16)


def group_conv(filter_rows, windows, shift, group_width, tail=None):
    taps = windows.shape[0] // 2
    lane = lax.broadcasted_iota(jnp.int32, (1, 2 * LANES), 1) % LANES // group_width
    total = jnp.zeros((taps, 2 * LANES), F32)
    end = None if tail is None else jnp.zeros((TAIL, LANES), F32)
    for g in range(LANES // group_width):
        band = toeplitz(filter_rows[g : g + 1, :], taps, shift)
        part = jnp.dot(band, windows, preferred_element_type=F32)
        total = jnp.where(lane == g, part, total)
        if tail is not None:
            part = jnp.dot(band[:16], tail, preferred_element_type=F32)[:TAIL]
            end = jnp.where(lane[:, :LANES] == g, part, end)
    joined = jnp.concatenate([total[:, :LANES], total[:, LANES:]], axis=0)
    return joined if tail is None else (joined, end)


def forward_kernel(group_width, feat_ref, taps_ref, filt_ref, halo_ref, conv_ref, mix_ref):
    rows = conv_ref.shape[0]
    taps = halo_ref.shape[0]
    pad = feat_ref.shape[1] - rows
    per = LANES // group_width
    for tile in range(conv_ref.shape[1] // LANES):
        cols = slice(tile * LANES, (tile + 1) * LANES)
        mixed = []
        for i in range(3):
            ext = feat_ref[i, :, cols].astype(F32)
            mixed.append(
                taps_ref[0, i : i + 1, cols] * ext[pad:]
                + taps_ref[1, i : i + 1, cols] * pltpu.roll(ext, 1, 0)[pad:]
                + taps_ref[2, i : i + 1, cols] * pltpu.roll(ext, 2, 0)[pad:]
            )
            mix_ref[i, :, cols] = mixed[i]
        products = (mixed[1] * mixed[2]).astype(BF16)
        whole = jnp.concatenate([halo_ref[:, cols], products], axis=0)
        windows = jnp.concatenate([whole[: 2 * taps], whole[taps : 3 * taps]], axis=1)
        conv_ref[:, cols] = group_conv(filt_ref[tile * per : (tile + 1) * per, :], windows, 1, group_width)


def backward_kernel(group_width, gc_ref, halo_ref, gg_ref, mix_ref, next_ref, taps_ref, filt_ref, out_ref):
    rows = gc_ref.shape[0]
    taps = filt_ref.shape[1] // 2
    held = halo_ref.shape[0]
    per = LANES // group_width
    for tile in range(gc_ref.shape[1] // LANES):
        cols = slice(tile * LANES, (tile + 1) * LANES)
        halo = halo_ref[:, cols]
        own = gc_ref[:, cols]
        last = jnp.concatenate([halo, jnp.zeros((2 * taps - held, LANES), BF16)], axis=0)
        windows = jnp.concatenate(
            [own, jnp.concatenate([own[taps:], halo[:taps]], axis=0)], axis=1
        )
        prod, prod_end = group_conv(filt_ref[tile * per : (tile + 1) * per, :], windows, 0, group_width, last)
        ends = (
            halo.astype(F32)[held - TAIL :],
            prod_end * next_ref[1, :, cols],
            prod_end * next_ref[0, :, cols],
        )
        bodies = (gg_ref[:, cols].astype(F32), prod * mix_ref[2, :, cols], prod * mix_ref[1, :, cols])
        for i in range(3):
            ext = jnp.concatenate([bodies[i], ends[i]], axis=0).astype(BF16).astype(F32)
            size = rows + TAIL
            out_ref[i, :, cols] = (
                taps_ref[0, i : i + 1, cols] * ext[:rows]
                + taps_ref[1, i : i + 1, cols] * pltpu.roll(ext, size - 1, 0)[:rows]
                + taps_ref[2, i : i + 1, cols] * pltpu.roll(ext, size - 2, 0)[:rows]
            ).astype(BF16)


def tiled(kernel, operands, outs, channels, group_width, flops, wide=512):
    wide = min(wide, channels)

    def spec(shape, by_group):
        if by_group:
            return pl.BlockSpec((wide // group_width,) + shape[1:], lambda c: (c, 0))
        lead = len(shape) - 1
        return pl.BlockSpec(shape[:-1] + (wide,), lambda c: (0,) * lead + (c,))

    moved = sum(a.size * a.dtype.itemsize for a, _ in operands) + sum(4 * o.size for o in outs)
    return pl.pallas_call(
        functools.partial(kernel, group_width),
        grid=(channels // wide,),
        in_specs=[spec(a.shape, by_group) for a, by_group in operands],
        out_specs=[spec(o.shape, False) for o in outs],
        out_shape=outs,
        compiler_params=pltpu.CompilerParams(vmem_limit_bytes=48 * 1024 * 1024),
        cost_estimate=pl.CostEstimate(flops=flops, bytes_accessed=moved, transcendentals=0),
    )(*[a for a, _ in operands])


def local(features, short_taps, long_filters, out_weight, out_grad):
    feats, taps, filters = features[0], short_taps[0], long_filters[0]
    weight, cotangent = out_weight[0], out_grad[0]
    rows, _, channels = feats.shape
    reach, groups = filters.shape
    width = channels // groups
    outer, inner = split_of(lax.axis_size("ctx"))
    place = lax.axis_index("ctx")
    z, x = place // inner, place % inner
    tp_count, tp_place = lax.axis_size("tp"), lax.axis_index("tp")
    chunks = max(1, min(CHUNKS, channels // 512))
    piece = channels // chunks
    own_depth = weight.shape[1]
    depth = inner * own_depth

    full = jnp.zeros((rows, tp_count * cotangent.shape[1]), cotangent.dtype)
    full = lax.dynamic_update_slice(full, cotangent, (0, tp_place * cotangent.shape[1]))
    for s in range(1, tp_count):
        got = lax.ppermute(cotangent, "tp", [(i, (i + s) % tp_count) for i in range(tp_count)])
        full = lax.dynamic_update_slice(full, got, (0, (tp_place - s) % tp_count * cotangent.shape[1]))
    tokens = jnp.zeros((outer, rows, depth), cotangent.dtype)
    for s in range(outer):
        block = lax.dynamic_slice(full, (0, (z + s) % outer * depth), (rows, depth))
        if s:
            route = [
                (zz * inner + xx, (zz + s) % outer * inner + xx) for zz in range(outer) for xx in range(inner)
            ]
            block = lax.ppermute(block, "ctx", route)
        tokens = lax.dynamic_update_slice(tokens, block[None], ((z - s) % outer, 0, 0))
    tokens = tokens.reshape(outer * rows, inner, own_depth)
    order = [(x - s) % inner for s in range(inner)]
    tokens = jnp.concatenate(
        [lax.dynamic_slice_in_dim(tokens, o, 1, 1)[:, 0] for o in order], axis=1
    )

    tail_f = feats[rows - reach - 2 :].astype(F32)
    tail_mix = taps[0] * tail_f[2:] + taps[1] * tail_f[1:-1] + taps[2] * tail_f[:-2]
    prod_halo = ahead((tail_mix[:, 1] * tail_mix[:, 2]).astype(BF16), "ctx", 1)
    feat_halo = ahead(feats[rows - 2 :], "ctx", 1)
    ext = jnp.concatenate([jnp.zeros((14, 3, channels), BF16), feat_halo, feats], axis=0)
    ext = jnp.transpose(ext, (1, 0, 2))
    by_group = jnp.transpose(filters).astype(F32)
    blank = jnp.zeros((groups, reach), F32)
    backward_rows = jnp.concatenate([by_group, blank], axis=1)
    forward_rows = jnp.concatenate([by_group[:, ::-1], blank], axis=1)
    flops = 2 * groups * reach * 4 * reach * LANES
    conv, mix = tiled(
        forward_kernel,
        [(ext, False), (taps, False), (forward_rows, True), (prod_halo, False)],
        [jax.ShapeDtypeStruct((rows, channels), F32), jax.ShapeDtypeStruct((3, rows, channels), F32)],
        channels,
        width,
        flops,
    )
    next_mix = ahead(mix[1:, :TAIL], "ctx", -1)

    results = []
    for k in range(chunks):
        lo, hi = k * piece, (k + 1) * piece
        mine = weight[lo:hi]
        held = [mine]
        for s in range(1, inner):
            route = [
                (zz * inner + xx, zz * inner + (xx + s) % inner) for zz in range(outer) for xx in range(inner)
            ]
            held.append(lax.ppermute(mine, "ctx", route))
        joined = jnp.concatenate(held, axis=1)
        partial = jnp.einsum("tn,cn->tc", tokens, joined, preferred_element_type=F32).astype(BF16)
        partial = partial.reshape(outer, rows, piece)

        def part_for(d):
            return lax.dynamic_index_in_dim(partial, jnp.clip(d, 0, outer - 1), 0, False).astype(F32)

        grad_y = part_for(z)
        for sign in (1, -1):
            got = None
            for j in range(outer - 1):
                send = part_for(z + sign * (outer - 1 - j))
                if got is not None:
                    send = send + got.astype(F32)
                sources = range(j + 1) if sign == 1 else range(outer - 1 - j, outer)
                route = [(zz * inner + xx, (zz + sign) * inner + xx) for zz in sources for xx in range(inner)]
                got = lax.ppermute(send.astype(BF16), "ctx", route)
            grad_y = grad_y + got.astype(F32)
        grad_y = grad_y.astype(BF16).astype(F32)
        grad_gate = (grad_y * conv[:, lo:hi]).astype(BF16)
        grad_conv = (grad_y * mix[0, :, lo:hi]).astype(BF16)
        halo = ahead(jnp.concatenate([grad_conv[: reach + 8], grad_gate[:TAIL]], axis=0), "ctx", -1)
        (out,) = tiled(
            backward_kernel,
            [
                (grad_conv, False),
                (halo, False),
                (grad_gate, False),
                (mix[:, :, lo:hi], False),
                (next_mix[:, :, lo:hi], False),
                (taps[:, :, lo:hi], False),
                (backward_rows[lo // width : hi // width], True),
            ],
            [jax.ShapeDtypeStruct((3, rows, piece), BF16)],
            piece,
            width,
            flops // chunks,
        )
        count = lax.axis_size("pp")
        results.append(lax.ppermute(out, "pp", [(i, (i - 1) % count) for i in range(count)]))
    return jnp.transpose(jnp.concatenate(results, axis=2), (1, 0, 2))[None]


def solution(mesh):
    in_specs = (
        P("pp", "ctx", None, "tp"),
        P("pp", None, None, "tp"),
        P("pp", None, "tp"),
        P("pp", "tp", "ctx"),
        P("pp", "ctx", "tp"),
    )
    out_specs = P("pp", "ctx", None, "tp")
    return jax.shard_map(local, mesh=mesh, in_specs=in_specs, out_specs=out_specs, check_vma=False)
```

```python
import functools

import jax
import jax.numpy as jnp
from jax import lax
from jax.experimental import pallas as pl
from jax.experimental.pallas import tpu as pltpu
from jax.sharding import PartitionSpec as P

LANES = 128
TAIL = 8
CHUNKS = 4
WAVES = 2
F32 = jnp.float32
BF16 = jnp.bfloat16


def split_of(count):
    inner = 1
    while inner * inner * 4 <= count:
        inner *= 2
    return count // inner, inner


def ahead(block, axis, distance):
    devices = range(lax.axis_size(axis))
    return lax.ppermute(block, axis, [(i - distance, i) for i in devices if i - distance in devices])


def toeplitz(row, rows, shift):
    wide = jnp.broadcast_to(row, (rows, row.shape[1]))
    return pltpu.roll(wide, shift, 1, stride=1, stride_axis=0).astype(BF16)


def group_conv(filter_rows, windows, shift, group_width, tail=None):
    taps = windows.shape[0] // 2
    lane = lax.broadcasted_iota(jnp.int32, (1, 2 * LANES), 1) % LANES // group_width
    total = jnp.zeros((taps, 2 * LANES), F32)
    end = None if tail is None else jnp.zeros((TAIL, LANES), F32)
    for g in range(LANES // group_width):
        band = toeplitz(filter_rows[g : g + 1, :], taps, shift)
        part = jnp.dot(band, windows, preferred_element_type=F32)
        total = jnp.where(lane == g, part, total)
        if tail is not None:
            part = jnp.dot(band[:16], tail, preferred_element_type=F32)[:TAIL]
            end = jnp.where(lane[:, :LANES] == g, part, end)
    joined = jnp.concatenate([total[:, :LANES], total[:, LANES:]], axis=0)
    return joined if tail is None else (joined, end)


def forward_kernel(group_width, feat_ref, before_ref, after_ref, taps_ref, filt_ref, halo_ref, conv_ref, mix_ref):
    rows = conv_ref.shape[0]
    taps = halo_ref.shape[0]
    pad = before_ref.shape[1]
    per = LANES // group_width
    for tile in range(conv_ref.shape[1] // LANES):
        cols = slice(tile * LANES, (tile + 1) * LANES)
        mixed = []
        for i in range(3):
            ext = jnp.concatenate(
                [before_ref[i, :, cols], feat_ref[i, :, cols].astype(F32), after_ref[i, :, cols]], axis=0
            )
            mixed.append(
                taps_ref[0, i : i + 1, cols] * ext[pad:]
                + taps_ref[1, i : i + 1, cols] * pltpu.roll(ext, 1, 0)[pad:]
                + taps_ref[2, i : i + 1, cols] * pltpu.roll(ext, 2, 0)[pad:]
            )
            mix_ref[i, :, cols] = mixed[i]
        products = (mixed[1] * mixed[2])[:rows].astype(BF16)
        whole = jnp.concatenate([halo_ref[:, cols], products], axis=0)
        windows = jnp.concatenate([whole[: 2 * taps], whole[taps : 3 * taps]], axis=1)
        conv_ref[:, cols] = group_conv(filt_ref[tile * per : (tile + 1) * per, :], windows, 1, group_width)


def backward_kernel(group_width, grad_ref, halo_ref, conv_ref, mix_ref, taps_ref, filt_ref, out_ref):
    rows = grad_ref.shape[0]
    taps = filt_ref.shape[1] // 2
    held = halo_ref.shape[0]
    per = LANES // group_width
    for tile in range(grad_ref.shape[1] // LANES):
        cols = slice(tile * LANES, (tile + 1) * LANES)
        halo = halo_ref[:, cols]
        grad_y = grad_ref[:, cols].astype(F32)
        own = (grad_y * mix_ref[0, :rows, cols]).astype(BF16)
        last = jnp.concatenate([halo, jnp.zeros((2 * taps - held, LANES), BF16)], axis=0)
        windows = jnp.concatenate(
            [own, jnp.concatenate([own[taps:], halo[:taps]], axis=0)], axis=1
        )
        prod, prod_end = group_conv(filt_ref[tile * per : (tile + 1) * per, :], windows, 0, group_width, last)
        prod = jnp.concatenate([prod, prod_end], axis=0)
        grad_gate = jnp.concatenate([grad_y * conv_ref[:, cols], halo.astype(F32)[held - TAIL :]], axis=0)
        for i, term in enumerate((grad_gate, prod * mix_ref[2, :, cols], prod * mix_ref[1, :, cols])):
            ext = term.astype(BF16).astype(F32)
            size = rows + TAIL
            out_ref[i, :, cols] = (
                taps_ref[0, i : i + 1, cols] * ext[:rows]
                + taps_ref[1, i : i + 1, cols] * pltpu.roll(ext, size - 1, 0)[:rows]
                + taps_ref[2, i : i + 1, cols] * pltpu.roll(ext, size - 2, 0)[:rows]
            ).astype(BF16)


def tiled(kernel, operands, outs, channels, group_width, flops, wide=512):
    wide = min(wide, channels)

    def spec(shape, by_group, start):
        first = start // wide
        if by_group:
            return pl.BlockSpec((wide // group_width,) + shape[1:], lambda c: (first + c, 0))
        lead = len(shape) - 1
        return pl.BlockSpec(shape[:-1] + (wide,), lambda c: (0,) * lead + (first + c,))

    moved = sum(a.size * a.dtype.itemsize for a, _, _ in operands) + sum(4 * o.size for o in outs)
    return pl.pallas_call(
        functools.partial(kernel, group_width),
        grid=(channels // wide,),
        in_specs=[spec(a.shape, by_group, start) for a, by_group, start in operands],
        out_specs=[spec(o.shape, False, 0) for o in outs],
        out_shape=outs,
        compiler_params=pltpu.CompilerParams(vmem_limit_bytes=48 * 1024 * 1024),
        cost_estimate=pl.CostEstimate(flops=flops, bytes_accessed=moved, transcendentals=0),
    )(*[a for a, _, _ in operands])


def after(value, *others):
    return lax.optimization_barrier((value,) + others)[0]


def local(features, short_taps, long_filters, out_weight, out_grad):
    feats, taps, filters = features[0], short_taps[0], long_filters[0]
    weight, cotangent = out_weight[0], out_grad[0]
    rows, _, channels = feats.shape
    reach, groups = filters.shape
    width = channels // groups
    outer, inner = split_of(lax.axis_size("ctx"))
    place = lax.axis_index("ctx")
    z, x = place // inner, place % inner
    tp_count, tp_place = lax.axis_size("tp"), lax.axis_index("tp")
    chunks = max(1, min(CHUNKS, channels // 512))
    waves = min(WAVES, chunks)
    piece, stretch = channels // chunks, channels // waves
    own_depth = weight.shape[1]
    depth = inner * own_depth
    share = cotangent.shape[1]
    cells = [(zz, xx) for zz in range(outer) for xx in range(inner)]

    full = jnp.zeros((rows, tp_count * share), cotangent.dtype)
    full = lax.dynamic_update_slice(full, cotangent, (0, tp_place * share))
    for s in range(1, tp_count):
        got = lax.ppermute(cotangent, "tp", [(i, (i + s) % tp_count) for i in range(tp_count)])
        full = lax.dynamic_update_slice(full, got, (0, (tp_place - s) % tp_count * share))

    weights = []
    for w in range(waves):
        mine = weight[w * stretch : (w + 1) * stretch]
        held = [mine]
        for s in range(1, inner):
            route = [(zz * inner + xx, zz * inner + (xx + s) % inner) for zz, xx in cells]
            held.append(lax.ppermute(mine, "ctx", route))
        weights.append(held)

    tokens = []
    for s in range(outer):
        start = (z + s) % outer * depth
        block = jnp.concatenate(
            [
                lax.dynamic_slice(full, (0, start + (x - i) % inner * own_depth), (rows, own_depth))
                for i in range(inner)
            ],
            axis=1,
        )
        if s:
            route = [(zz * inner + xx, (zz + s) % outer * inner + xx) for zz, xx in cells]
            block = lax.ppermute(block, "ctx", route)
        tokens.append(block)

    streams = jnp.transpose(feats, (1, 0, 2))
    tail_f = streams[:, rows - reach - 2 :].astype(F32)
    by_tap = taps[:, :, None]
    tail_mix = by_tap[0] * tail_f[:, 2:] + by_tap[1] * tail_f[:, 1:-1] + by_tap[2] * tail_f[:, :-2]
    prod_tail = (tail_mix[1] * tail_mix[2]).astype(BF16)
    packed = jnp.concatenate([prod_tail] + [streams[i, rows - 2 :] for i in range(3)], axis=0)
    packed = ahead(packed, "ctx", 1)
    prod_halo = packed[:reach]
    before = jnp.pad(packed[reach:].reshape(3, 2, channels).astype(F32), ((0, 0), (TAIL - 2, 0), (0, 0)))
    behind = ahead(streams[:, :2], "ctx", -1)
    behind = jnp.pad(behind.astype(F32), ((0, 0), (0, TAIL - 2), (0, 0)))
    by_group = jnp.transpose(filters).astype(F32)
    blank = jnp.zeros((groups, reach), F32)
    backward_rows = jnp.concatenate([by_group, blank], axis=1)
    forward_rows = jnp.concatenate([by_group[:, ::-1], blank], axis=1)
    flops = 2 * groups * reach * 4 * reach * LANES
    conv, mix = tiled(
        forward_kernel,
        [
            (streams, False, 0),
            (before, False, 0),
            (behind, False, 0),
            (taps, False, 0),
            (forward_rows, True, 0),
            (prod_halo, False, 0),
        ],
        [jax.ShapeDtypeStruct((rows, channels), F32), jax.ShapeDtypeStruct((3, rows + TAIL, channels), F32)],
        channels,
        width,
        flops,
    )

    results = []
    halos = []
    gate_order = {}
    per_wave = chunks // waves
    for k in range(chunks):
        lo, hi = k * piece, (k + 1) * piece
        wave, at = k // per_wave, k % per_wave
        joined = jnp.concatenate([h[at * piece : (at + 1) * piece] for h in weights[wave]], axis=1)
        partial = [
            lax.optimization_barrier(
                jnp.einsum("tn,cn->tc", block, joined, preferred_element_type=F32).astype(BF16)
            )
            for block in tokens
        ]
        total = partial[0].astype(F32)
        for sign in (1, -1):
            got = None
            for j in range(outer - 1):
                send = partial[j + 1] if sign == 1 else partial[outer - 1 - j]
                if got is not None:
                    send = (send.astype(F32) + got.astype(F32)).astype(BF16)
                    if wave and j == outer - 2:
                        send = after(send, halos[k - per_wave])
                elif wave:
                    send = after(send, gate_order[wave - 1, at, sign])
                sources = range(j + 1) if sign == 1 else range(outer - 1 - j, outer)
                route = [(zz * inner + xx, (zz + sign) * inner + xx) for zz in sources for xx in range(inner)]
                got = lax.ppermute(send, "ctx", route)
                if j == outer - 3:
                    gate_order[wave, at, sign] = got
            total = total + got.astype(F32)
        grad_y = total.astype(BF16)
        if wave:
            grad_y = after(grad_y, results[k - per_wave])
        top = grad_y[: reach + 8].astype(F32)
        halo = jnp.concatenate(
            [
                (top * mix[0, : reach + 8, lo:hi]).astype(BF16),
                (top[:TAIL] * conv[:TAIL, lo:hi]).astype(BF16),
            ],
            axis=0,
        )
        halos.append(halo)
        halo = ahead(halo, "ctx", -1)
        (out,) = tiled(
            backward_kernel,
            [
                (grad_y, False, 0),
                (halo, False, 0),
                (conv, False, lo),
                (mix, False, lo),
                (taps, False, lo),
                (backward_rows, True, lo),
            ],
            [jax.ShapeDtypeStruct((3, rows, piece), BF16)],
            piece,
            width,
            flops // chunks,
        )
        count = lax.axis_size("pp")
        results.append(lax.ppermute(out, "pp", [(i, (i - 1) % count) for i in range(count)]))
    return jnp.transpose(jnp.concatenate(results, axis=2), (1, 0, 2))[None]


def solution(mesh):
    in_specs = (
        P("pp", "ctx", None, "tp"),
        P("pp", None, None, "tp"),
        P("pp", None, "tp"),
        P("pp", "tp", "ctx"),
        P("pp", "ctx", "tp"),
    )
    out_specs = P("pp", "ctx", None, "tp")
    return jax.shard_map(local, mesh=mesh, in_specs=in_specs, out_specs=out_specs, check_vma=False)
```

```python
import functools

import jax
import jax.numpy as jnp
from jax import lax
from jax.experimental import pallas as pl
from jax.experimental.pallas import tpu as pltpu
from jax.sharding import PartitionSpec as P

LANES = 128
TAIL = 8
CHUNKS = 4
WAVES = 2
F32 = jnp.float32
BF16 = jnp.bfloat16


def split_of(count):
    inner = 1
    while inner * inner * 4 <= count:
        inner *= 2
    return count // inner, inner


def ahead(block, axis, distance):
    devices = range(lax.axis_size(axis))
    return lax.ppermute(block, axis, [(i - distance, i) for i in devices if i - distance in devices])


def toeplitz(row, rows, shift):
    wide = jnp.broadcast_to(row, (rows, row.shape[1]))
    return pltpu.roll(wide, shift, 1, stride=1, stride_axis=0).astype(BF16)


def group_conv(filter_rows, windows, shift, group_width, tail=None):
    taps = windows.shape[0] // 2
    lane = lax.broadcasted_iota(jnp.int32, (1, 2 * LANES), 1) % LANES // group_width
    total = jnp.zeros((taps, 2 * LANES), F32)
    end = None if tail is None else jnp.zeros((TAIL, LANES), F32)
    for g in range(LANES // group_width):
        band = toeplitz(filter_rows[g : g + 1, :], taps, shift)
        part = jnp.dot(band, windows, preferred_element_type=F32)
        total = jnp.where(lane == g, part, total)
        if tail is not None:
            part = jnp.dot(band[:16], tail, preferred_element_type=F32)[:TAIL]
            end = jnp.where(lane[:, :LANES] == g, part, end)
    joined = jnp.concatenate([total[:, :LANES], total[:, LANES:]], axis=0)
    return joined if tail is None else (joined, end)


def forward_kernel(group_width, feat_ref, before_ref, after_ref, taps_ref, filt_ref, halo_ref, conv_ref, mix_ref):
    rows = conv_ref.shape[0]
    taps = halo_ref.shape[0]
    pad = before_ref.shape[1]
    per = LANES // group_width
    for tile in range(conv_ref.shape[1] // LANES):
        cols = slice(tile * LANES, (tile + 1) * LANES)
        mixed = []
        for i in range(3):
            ext = jnp.concatenate(
                [before_ref[i, :, cols], feat_ref[i, :, cols].astype(F32), after_ref[i, :, cols]], axis=0
            )
            mixed.append(
                taps_ref[0, i : i + 1, cols] * ext[pad:]
                + taps_ref[1, i : i + 1, cols] * pltpu.roll(ext, 1, 0)[pad:]
                + taps_ref[2, i : i + 1, cols] * pltpu.roll(ext, 2, 0)[pad:]
            )
            mix_ref[i, :, cols] = mixed[i]
        products = (mixed[1] * mixed[2])[:rows].astype(BF16)
        whole = jnp.concatenate([halo_ref[:, cols], products], axis=0)
        windows = jnp.concatenate([whole[: 2 * taps], whole[taps : 3 * taps]], axis=1)
        conv_ref[:, cols] = group_conv(filt_ref[tile * per : (tile + 1) * per, :], windows, 1, group_width)


def backward_kernel(group_width, grad_ref, halo_ref, conv_ref, mix_ref, taps_ref, filt_ref, out_ref):
    rows = grad_ref.shape[0]
    taps = filt_ref.shape[1] // 2
    held = halo_ref.shape[0]
    per = LANES // group_width
    for tile in range(grad_ref.shape[1] // LANES):
        cols = slice(tile * LANES, (tile + 1) * LANES)
        halo = halo_ref[:, cols]
        grad_y = grad_ref[:, cols].astype(F32)
        own = (grad_y * mix_ref[0, :rows, cols]).astype(BF16)
        last = jnp.concatenate([halo, jnp.zeros((2 * taps - held, LANES), BF16)], axis=0)
        windows = jnp.concatenate(
            [own, jnp.concatenate([own[taps:], halo[:taps]], axis=0)], axis=1
        )
        prod, prod_end = group_conv(filt_ref[tile * per : (tile + 1) * per, :], windows, 0, group_width, last)
        prod = jnp.concatenate([prod, prod_end], axis=0)
        grad_gate = jnp.concatenate([grad_y * conv_ref[:, cols], halo.astype(F32)[held - TAIL :]], axis=0)
        for i, term in enumerate((grad_gate, prod * mix_ref[2, :, cols], prod * mix_ref[1, :, cols])):
            ext = term.astype(BF16).astype(F32)
            size = rows + TAIL
            out_ref[i, :, cols] = (
                taps_ref[0, i : i + 1, cols] * ext[:rows]
                + taps_ref[1, i : i + 1, cols] * pltpu.roll(ext, size - 1, 0)[:rows]
                + taps_ref[2, i : i + 1, cols] * pltpu.roll(ext, size - 2, 0)[:rows]
            ).astype(BF16)


def tiled(kernel, operands, outs, channels, group_width, flops, wide=512):
    wide = min(wide, channels)

    def spec(shape, by_group, start):
        first = start // wide
        if by_group:
            return pl.BlockSpec((wide // group_width,) + shape[1:], lambda c: (first + c, 0))
        lead = len(shape) - 1
        return pl.BlockSpec(shape[:-1] + (wide,), lambda c: (0,) * lead + (first + c,))

    moved = sum(a.size * a.dtype.itemsize for a, _, _ in operands) + sum(4 * o.size for o in outs)
    return pl.pallas_call(
        functools.partial(kernel, group_width),
        grid=(channels // wide,),
        in_specs=[spec(a.shape, by_group, start) for a, by_group, start in operands],
        out_specs=[spec(o.shape, False, 0) for o in outs],
        out_shape=outs,
        compiler_params=pltpu.CompilerParams(vmem_limit_bytes=48 * 1024 * 1024),
        cost_estimate=pl.CostEstimate(flops=flops, bytes_accessed=moved, transcendentals=0),
    )(*[a for a, _, _ in operands])


def after(value, *others):
    return lax.optimization_barrier((value,) + others)[0]


def local(features, short_taps, long_filters, out_weight, out_grad):
    feats, taps, filters = features[0], short_taps[0], long_filters[0]
    weight, cotangent = out_weight[0], out_grad[0]
    rows, _, channels = feats.shape
    reach, groups = filters.shape
    width = channels // groups
    outer, inner = split_of(lax.axis_size("ctx"))
    place = lax.axis_index("ctx")
    z, x = place // inner, place % inner
    tp_count, tp_place = lax.axis_size("tp"), lax.axis_index("tp")
    chunks = max(1, min(CHUNKS, channels // 512))
    waves = min(WAVES, chunks)
    piece, stretch = channels // chunks, channels // waves
    own_depth = weight.shape[1]
    depth = inner * own_depth
    share = cotangent.shape[1]
    cells = [(zz, xx) for zz in range(outer) for xx in range(inner)]

    full = jnp.zeros((rows, tp_count * share), cotangent.dtype)
    full = lax.dynamic_update_slice(full, cotangent, (0, tp_place * share))
    for s in range(1, tp_count):
        got = lax.ppermute(cotangent, "tp", [(i, (i + s) % tp_count) for i in range(tp_count)])
        full = lax.dynamic_update_slice(full, got, (0, (tp_place - s) % tp_count * share))

    streams = jnp.transpose(feats, (1, 0, 2))
    tail_f = streams[:, rows - reach - 2 :].astype(F32)
    by_tap = taps[:, :, None]
    tail_mix = by_tap[0] * tail_f[:, 2:] + by_tap[1] * tail_f[:, 1:-1] + by_tap[2] * tail_f[:, :-2]
    prod_tail = (tail_mix[1] * tail_mix[2]).astype(BF16)
    packed = jnp.concatenate([prod_tail] + [streams[i, rows - 2 :] for i in range(3)], axis=0)
    arrived = ahead(packed, "ctx", 1)

    weights = []
    for w in range(waves):
        mine = weight[w * stretch : (w + 1) * stretch]
        mine = after(mine, weights[-1][-1] if w else packed)
        held = [mine]
        for s in range(1, inner):
            route = [(zz * inner + xx, zz * inner + (xx + s) % inner) for zz, xx in cells]
            held.append(lax.ppermute(mine, "ctx", route))
        weights.append(held)

    tokens = []
    for s in range(outer):
        start = (z + s) % outer * depth
        block = jnp.concatenate(
            [
                lax.dynamic_slice(full, (0, start + (x - i) % inner * own_depth), (rows, own_depth))
                for i in range(inner)
            ],
            axis=1,
        )
        if s:
            route = [(zz * inner + xx, (zz + s) % outer * inner + xx) for zz, xx in cells]
            block = lax.ppermute(block, "ctx", route)
        tokens.append(block)

    prod_halo = arrived[:reach]
    before = jnp.pad(arrived[reach:].reshape(3, 2, channels).astype(F32), ((0, 0), (TAIL - 2, 0), (0, 0)))
    behind = ahead(streams[:, :2], "ctx", -1)
    behind = jnp.pad(behind.astype(F32), ((0, 0), (0, TAIL - 2), (0, 0)))
    by_group = jnp.transpose(filters).astype(F32)
    blank = jnp.zeros((groups, reach), F32)
    backward_rows = jnp.concatenate([by_group, blank], axis=1)
    forward_rows = jnp.concatenate([by_group[:, ::-1], blank], axis=1)
    flops = 2 * groups * reach * 4 * reach * LANES

    def forward(wave, *others):
        start = wave * stretch
        return tiled(
            forward_kernel,
            [
                (after(streams, *others), False, start),
                (before, False, start),
                (behind, False, start),
                (taps, False, start),
                (forward_rows, True, start),
                (prod_halo, False, start),
            ],
            [
                jax.ShapeDtypeStruct((rows, stretch), F32),
                jax.ShapeDtypeStruct((3, rows + TAIL, stretch), F32),
            ],
            stretch,
            width,
            flops // waves,
        )

    def partials(wave, at):
        joined = jnp.concatenate([h[at * piece : (at + 1) * piece] for h in weights[wave]], axis=1)
        return [
            lax.optimization_barrier(
                jnp.einsum("tn,cn->tc", block, joined, preferred_element_type=F32).astype(BF16)
            )
            for block in tokens
        ]

    results, halos = [], []
    per_wave = chunks // waves
    middle = [None] * per_wave
    every = [[partials(wave, at) for at in range(per_wave)] for wave in range(waves)]
    for wave in range(waves):
        parts = every[wave]
        conv, mix = forward(wave, *(middle[-1] if wave else parts[-1][1:]))
        sums = []
        for at in range(per_wave):
            total = parts[at][0].astype(F32)
            steps = []
            for sign in (1, -1):
                got = None
                for j in range(outer - 1):
                    send = parts[at][j + 1] if sign == 1 else parts[at][outer - 1 - j]
                    if got is not None:
                        send = (send.astype(F32) + got.astype(F32)).astype(BF16)
                        if wave and j == outer - 2:
                            send = after(send, halos[(wave - 1) * per_wave + at])
                        if wave + 1 < waves and j == outer - 2:
                            send = after(send, every[wave + 1][at][1], every[wave + 1][at][outer - 1])
                    elif wave:
                        send = after(send, middle[at][sign < 0])
                    sources = range(j + 1) if sign == 1 else range(outer - 1 - j, outer)
                    route = [(zz * inner + xx, (zz + sign) * inner + xx) for zz in sources for xx in range(inner)]
                    got = lax.ppermute(send, "ctx", route)
                    if j == max(0, outer - 3):
                        steps.append(got)
                total = total + got.astype(F32)
            middle[at] = steps
            sums.append(total.astype(BF16))
        ready = results[-per_wave:]
        for at in range(per_wave):
            lo = wave * stretch + at * piece
            here = slice(at * piece, (at + 1) * piece)
            grad_y = after(sums[at], ready[at]) if wave else sums[at]
            top = grad_y[: reach + 8].astype(F32)
            halo = jnp.concatenate(
                [
                    (top * mix[0, : reach + 8, here]).astype(BF16),
                    (top[:TAIL] * conv[:TAIL, here]).astype(BF16),
                ],
                axis=0,
            )
            halos.append(halo)
            halo = ahead(halo, "ctx", -1)
            (out,) = tiled(
                backward_kernel,
                [
                    (grad_y, False, 0),
                    (halo, False, 0),
                    (conv, False, at * piece),
                    (mix, False, at * piece),
                    (taps, False, lo),
                    (backward_rows, True, lo),
                ],
                [jax.ShapeDtypeStruct((3, rows, piece), BF16)],
                piece,
                width,
                flops // chunks,
            )
            count = lax.axis_size("pp")
            results.append(lax.ppermute(out, "pp", [(i, (i - 1) % count) for i in range(count)]))
    return jnp.transpose(jnp.concatenate(results, axis=2), (1, 0, 2))[None]


def solution(mesh):
    in_specs = (
        P("pp", "ctx", None, "tp"),
        P("pp", None, None, "tp"),
        P("pp", None, "tp"),
        P("pp", "tp", "ctx"),
        P("pp", "ctx", "tp"),
    )
    out_specs = P("pp", "ctx", None, "tp")
    return jax.shard_map(local, mesh=mesh, in_specs=in_specs, out_specs=out_specs, check_vma=False)
```

```python
import functools

import jax
import jax.numpy as jnp
from jax import lax
from jax.experimental import pallas as pl
from jax.experimental.pallas import tpu as pltpu
from jax.sharding import PartitionSpec as P

LANES = 128
TAIL = 8
CHUNKS = 4
WAVES = 2
F32 = jnp.float32
BF16 = jnp.bfloat16


def split_of(count):
    inner = 1
    while inner * inner * 4 <= count:
        inner *= 2
    return count // inner, inner


def ahead(block, axis, distance):
    devices = range(lax.axis_size(axis))
    return lax.ppermute(block, axis, [(i - distance, i) for i in devices if i - distance in devices])


def toeplitz(row, rows, shift):
    wide = jnp.broadcast_to(row, (rows, row.shape[1]))
    return pltpu.roll(wide, shift, 1, stride=1, stride_axis=0).astype(BF16)


def group_conv(filter_rows, windows, shift, group_width, tail=None):
    taps = windows.shape[0] // 2
    lane = lax.broadcasted_iota(jnp.int32, (1, 2 * LANES), 1) % LANES // group_width
    total = jnp.zeros((taps, 2 * LANES), F32)
    end = None if tail is None else jnp.zeros((TAIL, LANES), F32)
    for g in range(LANES // group_width):
        band = toeplitz(filter_rows[g : g + 1, :], taps, shift)
        part = jnp.dot(band, windows, preferred_element_type=F32)
        total = jnp.where(lane == g, part, total)
        if tail is not None:
            part = jnp.dot(band[:16], tail, preferred_element_type=F32)[:TAIL]
            end = jnp.where(lane[:, :LANES] == g, part, end)
    joined = jnp.concatenate([total[:, :LANES], total[:, LANES:]], axis=0)
    return joined if tail is None else (joined, end)


def forward_kernel(group_width, feat_ref, before_ref, after_ref, taps_ref, filt_ref, halo_ref, conv_ref, mix_ref):
    rows = conv_ref.shape[0]
    taps = halo_ref.shape[0]
    pad = before_ref.shape[1]
    per = LANES // group_width
    for tile in range(conv_ref.shape[1] // LANES):
        cols = slice(tile * LANES, (tile + 1) * LANES)
        mixed = []
        for i in range(3):
            ext = jnp.concatenate(
                [before_ref[i, :, cols], feat_ref[i, :, cols].astype(F32), after_ref[i, :, cols]], axis=0
            )
            mixed.append(
                taps_ref[0, i : i + 1, cols] * ext[pad:]
                + taps_ref[1, i : i + 1, cols] * pltpu.roll(ext, 1, 0)[pad:]
                + taps_ref[2, i : i + 1, cols] * pltpu.roll(ext, 2, 0)[pad:]
            )
            mix_ref[i, :, cols] = mixed[i]
        products = (mixed[1] * mixed[2])[:rows].astype(BF16)
        whole = jnp.concatenate([halo_ref[:, cols], products], axis=0)
        windows = jnp.concatenate([whole[: 2 * taps], whole[taps : 3 * taps]], axis=1)
        conv_ref[:, cols] = group_conv(filt_ref[tile * per : (tile + 1) * per, :], windows, 1, group_width)


def backward_kernel(group_width, grad_ref, halo_ref, conv_ref, mix_ref, taps_ref, filt_ref, out_ref):
    rows = grad_ref.shape[0]
    taps = filt_ref.shape[1] // 2
    held = halo_ref.shape[0]
    per = LANES // group_width
    for tile in range(grad_ref.shape[1] // LANES):
        cols = slice(tile * LANES, (tile + 1) * LANES)
        halo = halo_ref[:, cols]
        grad_y = grad_ref[:, cols].astype(F32)
        own = (grad_y * mix_ref[0, :rows, cols]).astype(BF16)
        last = jnp.concatenate([halo, jnp.zeros((2 * taps - held, LANES), BF16)], axis=0)
        windows = jnp.concatenate(
            [own, jnp.concatenate([own[taps:], halo[:taps]], axis=0)], axis=1
        )
        prod, prod_end = group_conv(filt_ref[tile * per : (tile + 1) * per, :], windows, 0, group_width, last)
        prod = jnp.concatenate([prod, prod_end], axis=0)
        grad_gate = jnp.concatenate([grad_y * conv_ref[:, cols], halo.astype(F32)[held - TAIL :]], axis=0)
        for i, term in enumerate((grad_gate, prod * mix_ref[2, :, cols], prod * mix_ref[1, :, cols])):
            ext = term.astype(BF16).astype(F32)
            size = rows + TAIL
            out_ref[i, :, cols] = (
                taps_ref[0, i : i + 1, cols] * ext[:rows]
                + taps_ref[1, i : i + 1, cols] * pltpu.roll(ext, size - 1, 0)[:rows]
                + taps_ref[2, i : i + 1, cols] * pltpu.roll(ext, size - 2, 0)[:rows]
            ).astype(BF16)


def tiled(kernel, operands, outs, channels, group_width, flops, wide=512):
    wide = min(wide, channels)

    def spec(shape, by_group, start):
        first = start // wide
        if by_group:
            return pl.BlockSpec((wide // group_width,) + shape[1:], lambda c: (first + c, 0))
        lead = len(shape) - 1
        return pl.BlockSpec(shape[:-1] + (wide,), lambda c: (0,) * lead + (first + c,))

    moved = sum(a.size * a.dtype.itemsize for a, _, _ in operands) + sum(4 * o.size for o in outs)
    return pl.pallas_call(
        functools.partial(kernel, group_width),
        grid=(channels // wide,),
        in_specs=[spec(a.shape, by_group, start) for a, by_group, start in operands],
        out_specs=[spec(o.shape, False, 0) for o in outs],
        out_shape=outs,
        compiler_params=pltpu.CompilerParams(vmem_limit_bytes=48 * 1024 * 1024),
        cost_estimate=pl.CostEstimate(flops=flops, bytes_accessed=moved, transcendentals=0),
    )(*[a for a, _, _ in operands])


def after(value, *others):
    return lax.optimization_barrier((value,) + others)[0]


def local(features, short_taps, long_filters, out_weight, out_grad):
    feats, taps, filters = features[0], short_taps[0], long_filters[0]
    weight, cotangent = out_weight[0], out_grad[0]
    rows, _, channels = feats.shape
    reach, groups = filters.shape
    width = channels // groups
    outer, inner = split_of(lax.axis_size("ctx"))
    place = lax.axis_index("ctx")
    z, x = place // inner, place % inner
    tp_count, tp_place = lax.axis_size("tp"), lax.axis_index("tp")
    chunks = max(1, min(CHUNKS, channels // 512))
    waves = min(WAVES, chunks)
    piece, stretch = channels // chunks, channels // waves
    own_depth = weight.shape[1]
    depth = inner * own_depth
    share = cotangent.shape[1]
    cells = [(zz, xx) for zz in range(outer) for xx in range(inner)]

    full = jnp.zeros((rows, tp_count * share), cotangent.dtype)
    full = lax.dynamic_update_slice(full, cotangent, (0, tp_place * share))
    for s in range(1, tp_count):
        got = lax.ppermute(cotangent, "tp", [(i, (i + s) % tp_count) for i in range(tp_count)])
        full = lax.dynamic_update_slice(full, got, (0, (tp_place - s) % tp_count * share))

    def spread(mine):
        held = [mine]
        for s in range(1, inner):
            route = [(zz * inner + xx, zz * inner + (xx + s) % inner) for zz, xx in cells]
            held.append(lax.ppermute(mine, "ctx", route))
        return held

    first = weight[:stretch]
    weights = [spread(first)]

    streams = jnp.transpose(feats, (1, 0, 2))
    tail_f = after(streams[:, rows - reach - 2 :], first).astype(F32)
    by_tap = taps[:, :, None]
    tail_mix = by_tap[0] * tail_f[:, 2:] + by_tap[1] * tail_f[:, 1:-1] + by_tap[2] * tail_f[:, :-2]
    prod_tail = (tail_mix[1] * tail_mix[2]).astype(BF16)
    packed = jnp.concatenate([prod_tail] + [streams[i, rows - 2 :] for i in range(3)], axis=0)
    arrived = ahead(packed, "ctx", 1)
    for w in range(1, waves):
        mine = weight[w * stretch : (w + 1) * stretch]
        weights.append(spread(after(mine, weights[-1][-1] if w > 1 else arrived)))

    tokens = []
    for s in range(outer):
        start = (z + s) % outer * depth
        block = jnp.concatenate(
            [
                lax.dynamic_slice(full, (0, start + (x - i) % inner * own_depth), (rows, own_depth))
                for i in range(inner)
            ],
            axis=1,
        )
        if s:
            route = [(zz * inner + xx, (zz + s) % outer * inner + xx) for zz, xx in cells]
            block = lax.ppermute(block, "ctx", route)
        tokens.append(block)

    prod_halo = arrived[:reach]
    before = jnp.pad(arrived[reach:].reshape(3, 2, channels).astype(F32), ((0, 0), (TAIL - 2, 0), (0, 0)))
    behind = ahead(streams[:, :2], "ctx", -1)
    behind = jnp.pad(behind.astype(F32), ((0, 0), (0, TAIL - 2), (0, 0)))
    by_group = jnp.transpose(filters).astype(F32)
    blank = jnp.zeros((groups, reach), F32)
    backward_rows = jnp.concatenate([by_group, blank], axis=1)
    forward_rows = jnp.concatenate([by_group[:, ::-1], blank], axis=1)
    flops = 2 * groups * reach * 4 * reach * LANES

    def forward(wave, *others):
        start = wave * stretch
        return tiled(
            forward_kernel,
            [
                (after(streams, *others), False, start),
                (before, False, start),
                (behind, False, start),
                (taps, False, start),
                (forward_rows, True, start),
                (prod_halo, False, start),
            ],
            [
                jax.ShapeDtypeStruct((rows, stretch), F32),
                jax.ShapeDtypeStruct((3, rows + TAIL, stretch), F32),
            ],
            stretch,
            width,
            flops // waves,
        )

    def partials(wave, at):
        joined = jnp.concatenate([h[at * piece : (at + 1) * piece] for h in weights[wave]], axis=1)
        return [
            lax.optimization_barrier(
                jnp.einsum("tn,cn->tc", block, joined, preferred_element_type=F32).astype(BF16)
            )
            for block in tokens
        ]

    results, halos = [], []
    per_wave = chunks // waves
    middle = [None] * per_wave
    every = [[partials(wave, at) for at in range(per_wave)] for wave in range(waves)]
    for wave in range(waves):
        parts = every[wave]
        conv, mix = forward(wave, *(middle[-1] if wave else parts[-1][1:]))
        sums = []
        for at in range(per_wave):
            total = parts[at][0].astype(F32)
            steps = []
            for sign in (1, -1):
                got = None
                for j in range(outer - 1):
                    send = parts[at][j + 1] if sign == 1 else parts[at][outer - 1 - j]
                    if got is not None:
                        send = (send.astype(F32) + got.astype(F32)).astype(BF16)
                        if wave and j == outer - 2:
                            send = after(send, halos[(wave - 1) * per_wave + at])
                        if wave + 1 < waves and j == outer - 2:
                            send = after(send, every[wave + 1][at][1], every[wave + 1][at][outer - 1])
                    elif wave:
                        send = after(send, middle[at][sign < 0])
                    sources = range(j + 1) if sign == 1 else range(outer - 1 - j, outer)
                    route = [(zz * inner + xx, (zz + sign) * inner + xx) for zz in sources for xx in range(inner)]
                    got = lax.ppermute(send, "ctx", route)
                    if j == max(0, outer - 3):
                        steps.append(got)
                total = total + got.astype(F32)
            middle[at] = steps
            sums.append(total.astype(BF16))
        ready = results[-per_wave:]
        for at in range(per_wave):
            lo = wave * stretch + at * piece
            here = slice(at * piece, (at + 1) * piece)
            grad_y = after(sums[at], ready[at]) if wave else sums[at]
            if at:
                grad_y = after(grad_y, halos[-1])
            top = grad_y[: reach + 8].astype(F32)
            halo = jnp.concatenate(
                [
                    (top * mix[0, : reach + 8, here]).astype(BF16),
                    (top[:TAIL] * conv[:TAIL, here]).astype(BF16),
                ],
                axis=0,
            )
            halos.append(halo)
            halo = ahead(halo, "ctx", -1)
            (out,) = tiled(
                backward_kernel,
                [
                    (grad_y, False, 0),
                    (halo, False, 0),
                    (conv, False, at * piece),
                    (mix, False, at * piece),
                    (taps, False, lo),
                    (backward_rows, True, lo),
                ],
                [jax.ShapeDtypeStruct((3, rows, piece), BF16)],
                piece,
                width,
                flops // chunks,
            )
            count = lax.axis_size("pp")
            results.append(lax.ppermute(out, "pp", [(i, (i - 1) % count) for i in range(count)]))
    return jnp.transpose(jnp.concatenate(results, axis=2), (1, 0, 2))[None]


def solution(mesh):
    in_specs = (
        P("pp", "ctx", None, "tp"),
        P("pp", None, None, "tp"),
        P("pp", None, "tp"),
        P("pp", "tp", "ctx"),
        P("pp", "ctx", "tp"),
    )
    out_specs = P("pp", "ctx", None, "tp")
    return jax.shard_map(local, mesh=mesh, in_specs=in_specs, out_specs=out_specs, check_vma=False)
```

```python
import functools

import jax
import jax.numpy as jnp
from jax import lax
from jax.experimental import pallas as pl
from jax.experimental.pallas import tpu as pltpu
from jax.sharding import PartitionSpec as P

LANES = 128
TAIL = 8
CHUNKS = 4
WAVES = 2
F32 = jnp.float32
BF16 = jnp.bfloat16


def split_of(count):
    inner = 1
    while inner * inner * 4 <= count:
        inner *= 2
    return count // inner, inner


def ahead(block, axis, distance):
    devices = range(lax.axis_size(axis))
    return lax.ppermute(block, axis, [(i - distance, i) for i in devices if i - distance in devices])


def toeplitz(row, rows, shift):
    wide = jnp.broadcast_to(row, (rows, row.shape[1]))
    return pltpu.roll(wide, shift, 1, stride=1, stride_axis=0).astype(BF16)


def group_conv(filter_rows, windows, shift, group_width, tail=None):
    taps = windows.shape[0] // 2
    lane = lax.broadcasted_iota(jnp.int32, (1, 2 * LANES), 1) % LANES // group_width
    total = jnp.zeros((taps, 2 * LANES), F32)
    end = None if tail is None else jnp.zeros((TAIL, LANES), F32)
    for g in range(LANES // group_width):
        band = toeplitz(filter_rows[g : g + 1, :], taps, shift)
        part = jnp.dot(band, windows, preferred_element_type=F32)
        total = jnp.where(lane == g, part, total)
        if tail is not None:
            part = jnp.dot(band[:16], tail, preferred_element_type=F32)[:TAIL]
            end = jnp.where(lane[:, :LANES] == g, part, end)
    joined = jnp.concatenate([total[:, :LANES], total[:, LANES:]], axis=0)
    return joined if tail is None else (joined, end)


def forward_kernel(group_width, feat_ref, before_ref, after_ref, taps_ref, filt_ref, halo_ref, conv_ref, mix_ref):
    rows = conv_ref.shape[0]
    taps = halo_ref.shape[0]
    pad = before_ref.shape[1]
    per = LANES // group_width
    for tile in range(conv_ref.shape[1] // LANES):
        cols = slice(tile * LANES, (tile + 1) * LANES)
        mixed = []
        for i in range(3):
            ext = jnp.concatenate(
                [before_ref[i, :, cols], feat_ref[i, :, cols].astype(F32), after_ref[i, :, cols]], axis=0
            )
            mixed.append(
                taps_ref[0, i : i + 1, cols] * ext[pad:]
                + taps_ref[1, i : i + 1, cols] * pltpu.roll(ext, 1, 0)[pad:]
                + taps_ref[2, i : i + 1, cols] * pltpu.roll(ext, 2, 0)[pad:]
            )
            mix_ref[i, :, cols] = mixed[i]
        products = (mixed[1] * mixed[2])[:rows].astype(BF16)
        whole = jnp.concatenate([halo_ref[:, cols], products], axis=0)
        windows = jnp.concatenate([whole[: 2 * taps], whole[taps : 3 * taps]], axis=1)
        conv_ref[:, cols] = group_conv(filt_ref[tile * per : (tile + 1) * per, :], windows, 1, group_width)


def backward_kernel(group_width, grad_ref, halo_ref, conv_ref, mix_ref, taps_ref, filt_ref, out_ref):
    rows = grad_ref.shape[0]
    taps = filt_ref.shape[1] // 2
    held = halo_ref.shape[0]
    per = LANES // group_width
    for tile in range(grad_ref.shape[1] // LANES):
        cols = slice(tile * LANES, (tile + 1) * LANES)
        halo = halo_ref[:, cols]
        grad_y = grad_ref[:, cols].astype(F32)
        own = (grad_y * mix_ref[0, :rows, cols]).astype(BF16)
        last = jnp.concatenate([halo, jnp.zeros((2 * taps - held, LANES), BF16)], axis=0)
        windows = jnp.concatenate(
            [own, jnp.concatenate([own[taps:], halo[:taps]], axis=0)], axis=1
        )
        prod, prod_end = group_conv(filt_ref[tile * per : (tile + 1) * per, :], windows, 0, group_width, last)
        prod = jnp.concatenate([prod, prod_end], axis=0)
        grad_gate = jnp.concatenate([grad_y * conv_ref[:, cols], halo.astype(F32)[held - TAIL :]], axis=0)
        for i, term in enumerate((grad_gate, prod * mix_ref[2, :, cols], prod * mix_ref[1, :, cols])):
            ext = term.astype(BF16).astype(F32)
            size = rows + TAIL
            out_ref[i, :, cols] = (
                taps_ref[0, i : i + 1, cols] * ext[:rows]
                + taps_ref[1, i : i + 1, cols] * pltpu.roll(ext, size - 1, 0)[:rows]
                + taps_ref[2, i : i + 1, cols] * pltpu.roll(ext, size - 2, 0)[:rows]
            ).astype(BF16)


def tiled(kernel, operands, outs, channels, group_width, flops, wide=512):
    wide = min(wide, channels)

    def spec(shape, by_group, start):
        first = start // wide
        if by_group:
            return pl.BlockSpec((wide // group_width,) + shape[1:], lambda c: (first + c, 0))
        lead = len(shape) - 1
        return pl.BlockSpec(shape[:-1] + (wide,), lambda c: (0,) * lead + (first + c,))

    moved = sum(a.size * a.dtype.itemsize for a, _, _ in operands) + sum(4 * o.size for o in outs)
    return pl.pallas_call(
        functools.partial(kernel, group_width),
        grid=(channels // wide,),
        in_specs=[spec(a.shape, by_group, start) for a, by_group, start in operands],
        out_specs=[spec(o.shape, False, 0) for o in outs],
        out_shape=outs,
        compiler_params=pltpu.CompilerParams(vmem_limit_bytes=48 * 1024 * 1024),
        cost_estimate=pl.CostEstimate(flops=flops, bytes_accessed=moved, transcendentals=0),
    )(*[a for a, _, _ in operands])


def after(value, *others):
    return lax.optimization_barrier((value,) + others)[0]


def local(features, short_taps, long_filters, out_weight, out_grad):
    feats, taps, filters = features[0], short_taps[0], long_filters[0]
    weight, cotangent = out_weight[0], out_grad[0]
    rows, _, channels = feats.shape
    reach, groups = filters.shape
    width = channels // groups
    outer, inner = split_of(lax.axis_size("ctx"))
    place = lax.axis_index("ctx")
    z, x = place // inner, place % inner
    tp_count, tp_place = lax.axis_size("tp"), lax.axis_index("tp")
    chunks = max(1, min(CHUNKS, channels // 512))
    waves = min(WAVES, chunks)
    piece, stretch = channels // chunks, channels // waves
    own_depth = weight.shape[1]
    depth = inner * own_depth
    share = cotangent.shape[1]
    cells = [(zz, xx) for zz in range(outer) for xx in range(inner)]

    full = jnp.zeros((rows, tp_count * share), cotangent.dtype)
    full = lax.dynamic_update_slice(full, cotangent, (0, tp_place * share))
    for s in range(1, tp_count):
        got = lax.ppermute(cotangent, "tp", [(i, (i + s) % tp_count) for i in range(tp_count)])
        full = lax.dynamic_update_slice(full, got, (0, (tp_place - s) % tp_count * share))

    streams = jnp.transpose(feats, (1, 0, 2))
    opening = streams[:, :2]
    behind = ahead(opening, "ctx", -1)
    tail_f = streams[:, rows - reach - 2 :].astype(F32)
    by_tap = taps[:, :, None]
    tail_mix = by_tap[0] * tail_f[:, 2:] + by_tap[1] * tail_f[:, 1:-1] + by_tap[2] * tail_f[:, :-2]
    prod_tail = (tail_mix[1] * tail_mix[2]).astype(BF16)
    packed = jnp.concatenate([prod_tail] + [streams[i, rows - 2 :] for i in range(3)], axis=0)
    arrived = ahead(packed, "ctx", 1)

    def spread(mine):
        held = [mine]
        for s in range(1, inner):
            route = [(zz * inner + xx, zz * inner + (xx + s) % inner) for zz, xx in cells]
            held.append(lax.ppermute(mine, "ctx", route))
        return held

    weights = []
    for w in range(waves):
        mine = weight[w * stretch : (w + 1) * stretch]
        weights.append(spread(after(mine, weights[-1][-1]) if w else after(mine, opening, packed)))

    tokens = []
    for s in range(outer):
        start = (z + s) % outer * depth
        block = jnp.concatenate(
            [
                lax.dynamic_slice(full, (0, start + (x - i) % inner * own_depth), (rows, own_depth))
                for i in range(inner)
            ],
            axis=1,
        )
        if s:
            route = [(zz * inner + xx, (zz + s) % outer * inner + xx) for zz, xx in cells]
            block = lax.ppermute(block, "ctx", route)
        tokens.append(block)

    by_group = jnp.transpose(filters).astype(F32)
    blank = jnp.zeros((groups, reach), F32)
    backward_rows = jnp.concatenate([by_group, blank], axis=1)
    forward_rows = jnp.concatenate([by_group[:, ::-1], blank], axis=1)
    flops = 2 * groups * reach * 4 * reach * LANES

    def forward(wave, *others):
        start = wave * stretch
        body, past, coming = lax.optimization_barrier((streams, arrived, behind) + others)[:3]
        prod_halo = past[:reach]
        before = past[reach:].reshape(3, 2, channels).astype(F32)
        before = jnp.pad(before, ((0, 0), (TAIL - 2, 0), (0, 0)))
        coming = jnp.pad(coming.astype(F32), ((0, 0), (0, TAIL - 2), (0, 0)))
        return tiled(
            forward_kernel,
            [
                (body, False, start),
                (before, False, start),
                (coming, False, start),
                (taps, False, start),
                (forward_rows, True, start),
                (prod_halo, False, start),
            ],
            [
                jax.ShapeDtypeStruct((rows, stretch), F32),
                jax.ShapeDtypeStruct((3, rows + TAIL, stretch), F32),
            ],
            stretch,
            width,
            flops // waves,
        )

    def partials(wave):
        joined = jnp.concatenate(weights[wave], axis=1)
        return [
            lax.optimization_barrier(
                jnp.einsum("tn,cn->tc", block, joined, preferred_element_type=F32).astype(BF16)
            )
            for block in tokens
        ]

    def hop(block, sign, far, sources):
        route = [(zz * inner + xx, (zz + sign * far) * inner + xx) for zz in sources for xx in range(inner)]
        return lax.ppermute(block, "ctx", route)

    def added(one, other):
        return (one.astype(F32) + other.astype(F32)).astype(BF16)

    def summed(part, sign, previous, held, steps):
        toward = part if sign == -1 else part[:1] + part[:0:-1]
        start = (lambda block: block) if previous is None else (lambda block: after(block, previous[sign < 0]))
        if outer == 4:
            end = 0 if sign == 1 else outer - 1
            far = hop(start(toward[3]), sign, 1, [end])
            near = hop(start(toward[1]), sign, 1, [zz for zz in range(outer) if 0 <= zz + sign < outer])
            both = added(toward[2], far)
            if held:
                both = after(both, *held)
            steps.append(near)
            return [near, hop(both, sign, 2, [zz for zz in range(outer) if 0 <= zz + 2 * sign < outer])]
        got = None
        for j in range(outer - 1):
            send = toward[outer - 1 - j]
            send = start(send) if got is None else added(send, got)
            if held and j == outer - 2:
                send = after(send, *held)
            got = hop(send, sign, 1, range(j + 1) if sign == 1 else range(outer - 1 - j, outer))
            if j == max(0, outer - 3):
                steps.append(got)
        return [got]

    results, halos = [], []
    per_wave = chunks // waves
    parts = [partials(wave) for wave in range(waves)]
    middle = None
    for wave in range(waves):
        conv, mix = forward(wave, *(middle or parts[wave][1:]))
        total = parts[wave][0].astype(F32)
        held = halos[-per_wave:] if wave else []
        if wave + 1 < waves:
            held = held + [parts[wave + 1][1], parts[wave + 1][outer - 1]]
        steps = []
        for sign in (1, -1):
            for got in summed(parts[wave], sign, middle, held, steps):
                total = total + got.astype(F32)
        middle = steps
        total = total.astype(BF16)
        ready = results[-per_wave:]
        for at in range(per_wave):
            lo = wave * stretch + at * piece
            here = slice(at * piece, (at + 1) * piece)
            grad_y = total[:, here]
            grad_y = after(grad_y, ready[at]) if wave else grad_y
            if at:
                grad_y = after(grad_y, halos[-1])
            top = grad_y[: reach + 8].astype(F32)
            halo = jnp.concatenate(
                [
                    (top * mix[0, : reach + 8, here]).astype(BF16),
                    (top[:TAIL] * conv[:TAIL, here]).astype(BF16),
                ],
                axis=0,
            )
            halos.append(halo)
            halo = ahead(halo, "ctx", -1)
            (out,) = tiled(
                backward_kernel,
                [
                    (grad_y, False, 0),
                    (halo, False, 0),
                    (conv, False, at * piece),
                    (mix, False, at * piece),
                    (taps, False, lo),
                    (backward_rows, True, lo),
                ],
                [jax.ShapeDtypeStruct((3, rows, piece), BF16)],
                piece,
                width,
                flops // chunks,
            )
            count = lax.axis_size("pp")
            results.append(lax.ppermute(out, "pp", [(i, (i - 1) % count) for i in range(count)]))
    return jnp.transpose(jnp.concatenate(results, axis=2), (1, 0, 2))[None]


def solution(mesh):
    in_specs = (
        P("pp", "ctx", None, "tp"),
        P("pp", None, None, "tp"),
        P("pp", None, "tp"),
        P("pp", "tp", "ctx"),
        P("pp", "ctx", "tp"),
    )
    out_specs = P("pp", "ctx", None, "tp")
    return jax.shard_map(local, mesh=mesh, in_specs=in_specs, out_specs=out_specs, check_vma=False)
```

```python
import functools

import jax
import jax.numpy as jnp
from jax import lax
from jax.experimental import pallas as pl
from jax.experimental.pallas import tpu as pltpu
from jax.sharding import PartitionSpec as P

LANES = 128
TAIL = 8
CHUNKS = 4
WAVES = 2
F32 = jnp.float32
BF16 = jnp.bfloat16


def split_of(count):
    inner = 1
    while inner * inner * 4 <= count:
        inner *= 2
    return count // inner, inner


def ahead(block, axis, distance):
    devices = range(lax.axis_size(axis))
    return lax.ppermute(block, axis, [(i - distance, i) for i in devices if i - distance in devices])


def toeplitz(row, rows, shift):
    wide = jnp.broadcast_to(row, (rows, row.shape[1]))
    return pltpu.roll(wide, shift, 1, stride=1, stride_axis=0).astype(BF16)


def group_conv(filter_rows, windows, shift, group_width, tail=None):
    taps = windows.shape[0] // 2
    lane = lax.broadcasted_iota(jnp.int32, (1, 2 * LANES), 1) % LANES // group_width
    total = jnp.zeros((taps, 2 * LANES), F32)
    end = None if tail is None else jnp.zeros((TAIL, LANES), F32)
    for g in range(LANES // group_width):
        band = toeplitz(filter_rows[g : g + 1, :], taps, shift)
        part = jnp.dot(band, windows, preferred_element_type=F32)
        total = jnp.where(lane == g, part, total)
        if tail is not None:
            part = jnp.dot(band[:16], tail, preferred_element_type=F32)[:TAIL]
            end = jnp.where(lane[:, :LANES] == g, part, end)
    joined = jnp.concatenate([total[:, :LANES], total[:, LANES:]], axis=0)
    return joined if tail is None else (joined, end)


def forward_kernel(group_width, feat_ref, before_ref, after_ref, taps_ref, filt_ref, halo_ref, conv_ref, mix_ref):
    rows = conv_ref.shape[0]
    taps = halo_ref.shape[0]
    pad = before_ref.shape[1]
    per = LANES // group_width
    for tile in range(conv_ref.shape[1] // LANES):
        cols = slice(tile * LANES, (tile + 1) * LANES)
        mixed = []
        for i in range(3):
            ext = jnp.concatenate(
                [before_ref[i, :, cols], feat_ref[i, :, cols].astype(F32), after_ref[i, :, cols]], axis=0
            )
            mixed.append(
                taps_ref[0, i : i + 1, cols] * ext[pad:]
                + taps_ref[1, i : i + 1, cols] * pltpu.roll(ext, 1, 0)[pad:]
                + taps_ref[2, i : i + 1, cols] * pltpu.roll(ext, 2, 0)[pad:]
            )
            mix_ref[i, :, cols] = mixed[i]
        products = (mixed[1] * mixed[2])[:rows].astype(BF16)
        whole = jnp.concatenate([halo_ref[:, cols], products], axis=0)
        windows = jnp.concatenate([whole[: 2 * taps], whole[taps : 3 * taps]], axis=1)
        conv_ref[:, cols] = group_conv(filt_ref[tile * per : (tile + 1) * per, :], windows, 1, group_width)


def backward_kernel(group_width, grad_ref, halo_ref, conv_ref, mix_ref, taps_ref, filt_ref, out_ref):
    rows = grad_ref.shape[0]
    taps = filt_ref.shape[1] // 2
    held = halo_ref.shape[0]
    per = LANES // group_width
    for tile in range(grad_ref.shape[1] // LANES):
        cols = slice(tile * LANES, (tile + 1) * LANES)
        halo = halo_ref[:, cols]
        grad_y = grad_ref[:, cols].astype(F32)
        own = (grad_y * mix_ref[0, :rows, cols]).astype(BF16)
        last = jnp.concatenate([halo, jnp.zeros((2 * taps - held, LANES), BF16)], axis=0)
        windows = jnp.concatenate(
            [own, jnp.concatenate([own[taps:], halo[:taps]], axis=0)], axis=1
        )
        prod, prod_end = group_conv(filt_ref[tile * per : (tile + 1) * per, :], windows, 0, group_width, last)
        prod = jnp.concatenate([prod, prod_end], axis=0)
        grad_gate = jnp.concatenate([grad_y * conv_ref[:, cols], halo.astype(F32)[held - TAIL :]], axis=0)
        for i, term in enumerate((grad_gate, prod * mix_ref[2, :, cols], prod * mix_ref[1, :, cols])):
            ext = term.astype(BF16).astype(F32)
            size = rows + TAIL
            out_ref[i, :, cols] = (
                taps_ref[0, i : i + 1, cols] * ext[:rows]
                + taps_ref[1, i : i + 1, cols] * pltpu.roll(ext, size - 1, 0)[:rows]
                + taps_ref[2, i : i + 1, cols] * pltpu.roll(ext, size - 2, 0)[:rows]
            ).astype(BF16)


def tiled(kernel, operands, outs, channels, group_width, flops, wide=512):
    wide = min(wide, channels)

    def spec(shape, by_group, start):
        first = start // wide
        if by_group:
            return pl.BlockSpec((wide // group_width,) + shape[1:], lambda c: (first + c, 0))
        lead = len(shape) - 1
        return pl.BlockSpec(shape[:-1] + (wide,), lambda c: (0,) * lead + (first + c,))

    moved = sum(a.size * a.dtype.itemsize for a, _, _ in operands) + sum(4 * o.size for o in outs)
    return pl.pallas_call(
        functools.partial(kernel, group_width),
        grid=(channels // wide,),
        in_specs=[spec(a.shape, by_group, start) for a, by_group, start in operands],
        out_specs=[spec(o.shape, False, 0) for o in outs],
        out_shape=outs,
        compiler_params=pltpu.CompilerParams(vmem_limit_bytes=48 * 1024 * 1024),
        cost_estimate=pl.CostEstimate(flops=flops, bytes_accessed=moved, transcendentals=0),
    )(*[a for a, _, _ in operands])


def after(value, *others):
    return lax.optimization_barrier((value,) + others)[0]


def local(features, short_taps, long_filters, out_weight, out_grad):
    feats, taps, filters = features[0], short_taps[0], long_filters[0]
    weight, cotangent = out_weight[0], out_grad[0]
    rows, _, channels = feats.shape
    reach, groups = filters.shape
    width = channels // groups
    outer, inner = split_of(lax.axis_size("ctx"))
    place = lax.axis_index("ctx")
    z, x = place // inner, place % inner
    tp_count, tp_place = lax.axis_size("tp"), lax.axis_index("tp")
    chunks = max(1, min(CHUNKS, channels // 512))
    waves = min(WAVES, chunks)
    stretch = channels // waves
    own_depth = weight.shape[1]
    depth = inner * own_depth
    share = cotangent.shape[1]
    cells = [(zz, xx) for zz in range(outer) for xx in range(inner)]

    full = jnp.zeros((rows, tp_count * share), cotangent.dtype)
    full = lax.dynamic_update_slice(full, cotangent, (0, tp_place * share))
    for s in range(1, tp_count):
        got = lax.ppermute(cotangent, "tp", [(i, (i + s) % tp_count) for i in range(tp_count)])
        full = lax.dynamic_update_slice(full, got, (0, (tp_place - s) % tp_count * share))

    def spread(mine):
        held = [mine]
        for s in range(1, inner):
            route = [(zz * inner + xx, zz * inner + (xx + s) % inner) for zz, xx in cells]
            held.append(lax.ppermute(mine, "ctx", route))
        return held

    first = weight[:stretch]
    weights = [spread(first)]

    streams = jnp.transpose(feats, (1, 0, 2))
    tail_f = after(streams[:, rows - reach - 2 :], first).astype(F32)
    by_tap = taps[:, :, None]
    tail_mix = by_tap[0] * tail_f[:, 2:] + by_tap[1] * tail_f[:, 1:-1] + by_tap[2] * tail_f[:, :-2]
    prod_tail = (tail_mix[1] * tail_mix[2]).astype(BF16)
    packed = jnp.concatenate([prod_tail] + [streams[i, rows - 2 :] for i in range(3)], axis=0)
    arrived = ahead(packed, "ctx", 1)
    opening = after(streams[:, :2], weights[0][-1])
    behind = ahead(opening, "ctx", -1)
    for w in range(1, waves):
        weights.append(spread(after(weight[w * stretch : (w + 1) * stretch], opening, weights[-1][-1])))

    tokens = []
    for s in range(outer):
        start = (z + s) % outer * depth
        block = jnp.concatenate(
            [
                lax.dynamic_slice(full, (0, start + (x - i) % inner * own_depth), (rows, own_depth))
                for i in range(inner)
            ],
            axis=1,
        )
        if s:
            route = [(zz * inner + xx, (zz + s) % outer * inner + xx) for zz, xx in cells]
            block = lax.ppermute(block, "ctx", route)
        tokens.append(block)

    by_group = jnp.transpose(filters).astype(F32)
    blank = jnp.zeros((groups, reach), F32)
    backward_rows = jnp.concatenate([by_group, blank], axis=1)
    forward_rows = jnp.concatenate([by_group[:, ::-1], blank], axis=1)
    flops = 2 * groups * reach * 4 * reach * LANES

    def forward(wave, *others):
        start = wave * stretch
        body, past, coming = lax.optimization_barrier((streams, arrived, behind) + others)[:3]
        prod_halo = past[:reach]
        before = past[reach:].reshape(3, 2, channels).astype(F32)
        before = jnp.pad(before, ((0, 0), (TAIL - 2, 0), (0, 0)))
        coming = jnp.pad(coming.astype(F32), ((0, 0), (0, TAIL - 2), (0, 0)))
        return tiled(
            forward_kernel,
            [
                (body, False, start),
                (before, False, start),
                (coming, False, start),
                (taps, False, start),
                (forward_rows, True, start),
                (prod_halo, False, start),
            ],
            [
                jax.ShapeDtypeStruct((rows, stretch), F32),
                jax.ShapeDtypeStruct((3, rows + TAIL, stretch), F32),
            ],
            stretch,
            width,
            flops // waves,
        )

    def partials(wave):
        joined = jnp.concatenate(weights[wave], axis=1)
        return [
            lax.optimization_barrier(
                jnp.einsum("tn,cn->tc", block, joined, preferred_element_type=F32).astype(BF16)
            )
            for block in tokens
        ]

    def hop(block, sign, far, sources):
        route = [(zz * inner + xx, (zz + sign * far) * inner + xx) for zz in sources for xx in range(inner)]
        return lax.ppermute(block, "ctx", route)

    def added(one, other):
        return (one.astype(F32) + other.astype(F32)).astype(BF16)

    def summed(part, sign, previous, held, steps):
        toward = part if sign == -1 else part[:1] + part[:0:-1]
        start = (lambda block: block) if previous is None else (lambda block: after(block, previous[sign < 0]))
        if outer == 4:
            end = 0 if sign == 1 else outer - 1
            far = hop(toward[3], sign, 1, [end])
            near = hop(start(toward[1]), sign, 1, [zz for zz in range(outer) if 0 <= zz + sign < outer])
            both = added(toward[2], far)
            if held:
                both = after(both, *held)
            steps.append(near)
            return [near, hop(both, sign, 2, [zz for zz in range(outer) if 0 <= zz + 2 * sign < outer])]
        got = None
        for j in range(outer - 1):
            send = toward[outer - 1 - j]
            send = start(send) if got is None else added(send, got)
            if held and j == outer - 2:
                send = after(send, *held)
            got = hop(send, sign, 1, range(j + 1) if sign == 1 else range(outer - 1 - j, outer))
            if j == max(0, outer - 3):
                steps.append(got)
        return [got]

    results, halos = [], []
    per_wave = chunks // waves
    parts = [partials(wave) for wave in range(waves)]
    middle = None
    for wave in range(waves):
        conv, mix = forward(wave, *(middle or parts[wave][1:]))
        total = parts[wave][0].astype(F32)
        held = halos[-1:] if wave else []
        if wave + 1 < waves:
            held = held + [parts[wave + 1][1], parts[wave + 1][outer - 1]]
        steps = []
        for sign in (1, -1):
            for got in summed(parts[wave], sign, middle, held, steps):
                total = total + got.astype(F32)
        middle = steps
        total = total.astype(BF16)
        ready = results[-1:]
        count = per_wave if wave + 1 == waves else 1
        piece = stretch // count
        for at in range(count):
            lo = wave * stretch + at * piece
            here = slice(at * piece, (at + 1) * piece)
            grad_y = total[:, here]
            grad_y = after(grad_y, *ready) if wave else grad_y
            if at:
                grad_y = after(grad_y, halos[-1])
            top = grad_y[: reach + 8].astype(F32)
            halo = jnp.concatenate(
                [
                    (top * mix[0, : reach + 8, here]).astype(BF16),
                    (top[:TAIL] * conv[:TAIL, here]).astype(BF16),
                ],
                axis=0,
            )
            halos.append(halo)
            halo = ahead(halo, "ctx", -1)
            (out,) = tiled(
                backward_kernel,
                [
                    (grad_y, False, 0),
                    (halo, False, 0),
                    (conv, False, at * piece),
                    (mix, False, at * piece),
                    (taps, False, lo),
                    (backward_rows, True, lo),
                ],
                [jax.ShapeDtypeStruct((3, rows, piece), BF16)],
                piece,
                width,
                flops * piece // channels,
            )
            pages = lax.axis_size("pp")
            results.append(lax.ppermute(out, "pp", [(i, (i - 1) % pages) for i in range(pages)]))
    return jnp.transpose(jnp.concatenate(results, axis=2), (1, 0, 2))[None]


def solution(mesh):
    in_specs = (
        P("pp", "ctx", None, "tp"),
        P("pp", None, None, "tp"),
        P("pp", None, "tp"),
        P("pp", "tp", "ctx"),
        P("pp", "ctx", "tp"),
    )
    out_specs = P("pp", "ctx", None, "tp")
    return jax.shard_map(local, mesh=mesh, in_specs=in_specs, out_specs=out_specs, check_vma=False)
```
